128 devices in a mesh: subtree: 4 (over y), front: 32 (over z, x, core).
Axes of the slice: x: 4, y: 4, z: 4, core: 2. Of those that a mesh axis runs over, the one named last changes fastest.
Arguments:
- inverse_root: bfloat16 [12288, 12288], P('front', 'subtree'), may hold values from -0.0546875 to 0.0546875
- values_root: bfloat16 [12288, 512], P(('subtree', 'front')), may hold values from -6 to 6
- blocks_root: float32 [3, 6144], P(None, ('subtree', 'front')), may hold values from 0.5 to 1.5
- pairs_root: int32 [6144], P(('subtree', 'front')), may hold values from 0 to 1
- inverse_mid: bfloat16 [4, 8192, 8192], P('subtree', 'front'), may hold values from -0.0625 to 0.0625
- lower_mid: bfloat16 [4, 4096, 8192], P('subtree', None, 'front'), may hold values from -0.09375 to 0.09375
- values_mid: bfloat16 [4, 8192, 512], P('subtree', 'front'), may hold values from -6 to 6
- blocks_mid: float32 [4, 3, 4096], P('subtree', None, 'front'), may hold values from 0.5 to 1.5
- pairs_mid: int32 [4, 4096], P('subtree', 'front'), may hold values from 0 to 1
- rows_mid: int32 [4, 4096], P('subtree'), may hold values from 0 to 12287
- inverse_low: bfloat16 [128, 2048, 2048], P(('subtree', 'front')), may hold values from -0.125 to 0.125
- lower_low: bfloat16 [128, 1024, 2048], P(('subtree', 'front')), may hold values from -0.1875 to 0.1875
- lower_delay: bfloat16 [128, 128, 2048], P(('subtree', 'front')), may hold values from -0.5 to 0.5
- values_low: bfloat16 [128, 2048, 512], P(('subtree', 'front')), may hold values from -6 to 6
- blocks_low: float32 [128, 3, 1024], P(('subtree', 'front')), may hold values from 0.5 to 1.5
- pairs_low: int32 [128, 1024], P(('subtree', 'front')), may hold values from 0 to 1
- rows_low: int32 [128, 1024], P(('subtree', 'front')), may hold values from 0 to 20479
- delayed_low: int32 [128, 128], P(('subtree', 'front')), may hold values from 0 to 8191
Outputs:
- solved_root: bfloat16 [12288, 512], P(('subtree', 'front'))
- solved_mid: bfloat16 [4, 8192, 512], P('subtree', 'front')
- solved_low: bfloat16 [128, 2048, 512], P(('subtree', 'front'))
The draws below stay inside these ranges and needn't reach their ends.
All inputs are finite; a program needn't handle non-finite values.
Results may differ from the reference program's by a relative error of at most 0.012.
Values may be sent and summed in bfloat16 or wider, within the bound.
A program may use at most 192 MiB of HBM per device.

```python
import jax
import jax.numpy as jnp
from jax import lax

PIV_ROOT = 12288
PIV_MID = 8192
UPD_MID = 4096
PIV_LOW = 2048
UPD_LOW = 1024
DELAYED = 128
RHS = 512
MIDS = 4
CHILDREN = 32
LOWS = 128


def plant(values, own_key, low, largest):
    index_at = [jax.random.randint(jax.random.fold_in(own_key, axis), (), 0, length) for axis, length in enumerate(values.shape)]
    widest = values.shape.index(max(values.shape))
    next_to = index_at[:widest] + [(index_at[widest] + 1) % values.shape[widest]] + index_at[widest + 1:]
    return values.at[tuple(index_at)].set(low).at[tuple(next_to)].set(largest)


def levels(rng, extent, cuts, smallest, largest):
    def one(dim, parts):
        heights = jax.random.uniform(jax.random.fold_in(jax.random.fold_in(rng, 6), dim), (parts,), jnp.float32, smallest / len(cuts), largest / len(cuts))
        return jnp.repeat(jnp.exp(heights), extent[dim] // parts).reshape((-1,) + (1,) * (len(extent) - dim - 1))

    factor_of = one(*cuts[0])
    for cut in cuts[1:]:
        factor_of = factor_of * one(*cut)
    return factor_of


def normal_values(key, shape, deviation, limit, split=(), held_as=jnp.bfloat16):
    loudness = levels(key, shape, split, -0.22, 0.18) if split else 1.0
    values = jax.random.normal(key, shape, jnp.float32) * deviation * loudness
    return jnp.minimum(jnp.maximum(values, -limit), limit).astype(held_as)


def setup_inputs(seed: int = 0) -> dict:
    arg_keys = jax.random.split(jax.random.key(seed), 19)
    inverse_root = normal_values(arg_keys[0], (PIV_ROOT, PIV_ROOT), PIV_ROOT ** -0.5, 0.0546875, ((0, 32), (1, 4)))
    values_root = normal_values(arg_keys[1], (PIV_ROOT, RHS), 1.0, 6.0, ((0, 128),))
    blocks_root = jnp.clip(0.5 + 1.0 * jax.random.uniform(arg_keys[2], (3, PIV_ROOT // 2), jnp.float32) ** levels(arg_keys[2], (3, PIV_ROOT // 2), ((1, 128),), -0.2, 0.2), 0.5, 1.5)
    pairs_root = plant(jax.random.randint(arg_keys[3], (PIV_ROOT // 2,), 0, 2), jax.random.fold_in(arg_keys[3], 1), 0, 1).astype(jnp.int32)
    inverse_mid = normal_values(arg_keys[4], (MIDS, PIV_MID, PIV_MID), PIV_MID ** -0.5, 0.0625, ((0, 4), (1, 32)))
    lower_mid = normal_values(arg_keys[5], (MIDS, UPD_MID, PIV_MID), UPD_MID ** -0.5, 0.09375, ((0, 4), (2, 32)))
    values_mid = normal_values(arg_keys[6], (MIDS, PIV_MID, RHS), 1.0, 6.0, ((0, 4), (1, 32)))
    blocks_mid = jnp.clip(0.5 + 1.0 * jax.random.uniform(arg_keys[7], (MIDS, 3, PIV_MID // 2), jnp.float32) ** levels(arg_keys[7], (MIDS, 3, PIV_MID // 2), ((0, 4), (2, 32)), -0.2, 0.2), 0.5, 1.5)
    pairs_mid = plant(jax.random.randint(arg_keys[8], (MIDS, PIV_MID // 2), 0, 2), jax.random.fold_in(arg_keys[8], 1), 0, 1).astype(jnp.int32)
    rows_mid = plant(jax.random.randint(arg_keys[9], (MIDS, UPD_MID), 0, PIV_ROOT), jax.random.fold_in(arg_keys[9], 1), 0, PIV_ROOT - 1).astype(jnp.int32)
    inverse_low = normal_values(arg_keys[10], (LOWS, PIV_LOW, PIV_LOW), PIV_LOW ** -0.5, 0.125, ((0, 128),))
    lower_low = normal_values(arg_keys[11], (LOWS, UPD_LOW, PIV_LOW), UPD_LOW ** -0.5, 0.1875, ((0, 128),))
    lower_delay = normal_values(arg_keys[12], (LOWS, DELAYED, PIV_LOW), DELAYED ** -0.5, 0.5, ((0, 128),))
    values_low = normal_values(arg_keys[13], (LOWS, PIV_LOW, RHS), 1.0, 6.0, ((0, 128),))
    blocks_low = jnp.clip(0.5 + 1.0 * jax.random.uniform(arg_keys[14], (LOWS, 3, PIV_LOW // 2), jnp.float32) ** levels(arg_keys[14], (LOWS, 3, PIV_LOW // 2), ((0, 128),), -0.2, 0.2), 0.5, 1.5)
    pairs_low = plant(jax.random.randint(arg_keys[15], (LOWS, PIV_LOW // 2), 0, 2), jax.random.fold_in(arg_keys[15], 1), 0, 1).astype(jnp.int32)
    rows_low = plant(jax.random.randint(arg_keys[16], (LOWS, UPD_LOW), 0, PIV_ROOT + PIV_MID), jax.random.fold_in(arg_keys[16], 1), 0, (PIV_ROOT + PIV_MID) - 1).astype(jnp.int32)
    delayed_low = plant(jax.random.randint(arg_keys[17], (LOWS, DELAYED), 0, PIV_MID), jax.random.fold_in(arg_keys[17], 1), 0, PIV_MID - 1).astype(jnp.int32)
    return dict(inverse_root=inverse_root, values_root=values_root, blocks_root=blocks_root, pairs_root=pairs_root, inverse_mid=inverse_mid, lower_mid=lower_mid, values_mid=values_mid, blocks_mid=blocks_mid, pairs_mid=pairs_mid, rows_mid=rows_mid, inverse_low=inverse_low, lower_low=lower_low, lower_delay=lower_delay, values_low=values_low, blocks_low=blocks_low, pairs_low=pairs_low, rows_low=rows_low, delayed_low=delayed_low)


def scale_pivots(values, blocks, pair_flags):
    halves = values.shape[0] // 2
    paired = values.astype(jnp.float32).reshape(halves, 2, values.shape[1])
    linked = (pair_flags.astype(jnp.float32) * blocks[2])[:, None]
    leading = blocks[0][:, None] * paired[:, 0] + linked * paired[:, 1]
    trailing = blocks[1][:, None] * paired[:, 1] + linked * paired[:, 0]
    return jnp.stack([leading, trailing], axis=1).reshape(2 * halves, values.shape[1])


def reference(inverse_root, values_root, blocks_root, pairs_root, inverse_mid, lower_mid, values_mid, blocks_mid, pairs_mid, rows_mid, inverse_low, lower_low, lower_delay, values_low, blocks_low, pairs_low, rows_low, delayed_low):
    scaled_root = scale_pivots(values_root, blocks_root, pairs_root).astype(jnp.bfloat16)
    solved_root = jnp.dot(inverse_root, scaled_root, preferred_element_type=jnp.float32).astype(jnp.bfloat16)
    solved = []
    for member in range(MIDS):
        picked = jnp.take(solved_root, rows_mid[member], axis=0)
        update = jnp.dot(lower_mid[member].T, picked, preferred_element_type=jnp.float32)
        reduced = (scale_pivots(values_mid[member], blocks_mid[member], pairs_mid[member]) - update).astype(jnp.bfloat16)
        solved.append(jnp.dot(inverse_mid[member], reduced, preferred_element_type=jnp.float32).astype(jnp.bfloat16))
    solved_mid = jnp.stack(solved)
    parents = jnp.arange(LOWS, dtype=jnp.int32) // CHILDREN

    def one_front(operands):
        inverse, lower_part, delays, values, blocks, pair_flags, row_list, delayed, parent = operands
        ancestor = jnp.take(solved_mid, parent, axis=0)
        from_root = (row_list < PIV_ROOT)[:, None]
        root_pick = jnp.take(solved_root, jnp.minimum(row_list, PIV_ROOT - 1), axis=0)
        parent_pick = jnp.take(ancestor, jnp.maximum(row_list - PIV_ROOT, 0), axis=0)
        chosen = jnp.where(from_root, root_pick, parent_pick)
        update = jnp.dot(lower_part.T, chosen, preferred_element_type=jnp.float32)
        update = update + jnp.dot(delays.T, jnp.take(ancestor, delayed, axis=0), preferred_element_type=jnp.float32)
        reduced = (scale_pivots(values, blocks, pair_flags) - update).astype(jnp.bfloat16)
        return jnp.dot(inverse, reduced, preferred_element_type=jnp.float32).astype(jnp.bfloat16)

    solved_low = lax.map(one_front, (inverse_low, lower_low, lower_delay, values_low, blocks_low, pairs_low, rows_low, delayed_low, parents))
    return (solved_root, solved_mid, solved_low)
```

```python
import jax
import jax.numpy as jnp
from jax import lax
from jax.experimental import pallas as pl
from jax.experimental.pallas import tpu as pltpu
from jax.sharding import PartitionSpec as P

MESH = pl.DeviceIdType.MESH
F32, BF16 = jnp.float32, jnp.bfloat16
HALVES = 2
WIDE = 512 // HALVES
QUARTERS = WIDE // 128
ROOT = 12288
MID = 8192
UPD = 4096
LOW = 2048
PICK = 1024
DELAY = 128
GATHERS = 4
SLOTS = 24


def front_of(z, x, c):
    return (lax.rem(z, 4) * 4 + lax.rem(x, 4)) * 2 + lax.rem(c, 2)


class Here:
    def __init__(self):
        self.y = lax.axis_index("subtree")
        f = lax.axis_index("front")
        self.z = lax.div(f, 8)
        self.x = lax.rem(lax.div(f, 2), 4)
        self.c = lax.rem(f, 2)

    def front(self, dz=0, dx=0, dc=0):
        return (self.y, front_of(self.z + dz, self.x + dx, self.c + dc))

    def level(self, dy):
        return (lax.rem(self.y + dy, 4), front_of(self.z, self.x, self.c))


class PlaneGather:
    def __init__(self, here, buf, send, recv, parts):
        self.here, self.buf, self.send, self.recv, self.parts = here, buf, send, recv, parts

    def rows(self, p, sub):
        start, first, second = self.parts[p]
        if sub is None:
            return pl.ds(start, first + second)
        return pl.ds(start, first) if sub == 0 else pl.ds(start + first, second)

    def block(self, p, da, sub=None):
        h = self.here
        if p == 0:
            return self.buf.at[h.z, lax.rem(h.x + da, 4), h.c, self.rows(p, sub)]
        return self.buf.at[lax.rem(h.z + da, 4), h.x, h.c, self.rows(p, sub)]

    def slab(self, p, db, sub=None, dc=0):
        h = self.here
        c = lax.rem(h.c + dc, 2)
        if p == 0:
            return self.buf.at[lax.rem(h.z + db, 4), :, c, self.rows(p, sub)]
        return self.buf.at[:, lax.rem(h.x + db, 4), c, self.rows(p, sub)]

    def along(self, p, step):
        return self.here.front(dx=step) if p == 0 else self.here.front(dz=step)

    def across(self, p, step):
        return self.here.front(dz=step) if p == 0 else self.here.front(dx=step)

    def copy(self, ref, p, slot, target):
        return pltpu.make_async_remote_copy(
            src_ref=ref,
            dst_ref=ref,
            send_sem=self.send.at[p * 12 + slot],
            recv_sem=self.recv.at[p * 12 + slot],
            device_id=target,
            device_id_type=MESH,
        )

    def arrive(self, ref, p, slot):
        self.copy(ref, p, slot, self.here.front(dc=1)).wait_recv()

    def begin(self):
        for p in (0, 1):
            self.copy(self.block(p, 0), p, 0, self.along(p, 1)).start()
            self.copy(self.block(p, 0), p, 1, self.along(p, 3)).start()

    def hop2(self):
        for p in (0, 1):
            self.arrive(self.block(p, 3), p, 0)
            self.copy(self.block(p, 3, 0), p, 2, self.along(p, 1)).start()
            self.arrive(self.block(p, 1), p, 1)
            self.copy(self.block(p, 1, 1), p, 3, self.along(p, 3)).start()

    def hop3(self):
        for p in (0, 1):
            self.arrive(self.block(p, 2, 0), p, 2)
            self.arrive(self.block(p, 2, 1), p, 3)
            self.copy(self.slab(p, 0), p, 4, self.across(p, 1)).start()
            self.copy(self.slab(p, 0), p, 5, self.across(p, 3)).start()
        for p in (0, 1):
            self.copy(self.slab(p, 0), p, 8, self.here.front(dc=1)).start()

    def hop4(self):
        for p in (0, 1):
            self.arrive(self.slab(p, 3), p, 4)
            self.copy(self.slab(p, 3, 0), p, 6, self.across(p, 1)).start()
            self.arrive(self.slab(p, 1), p, 5)
            self.copy(self.slab(p, 1, 1), p, 7, self.across(p, 3)).start()
        for p in (0, 1):
            self.copy(self.slab(p, 3), p, 9, self.here.front(dc=1)).start()
            self.copy(self.slab(p, 1), p, 10, self.here.front(dc=1)).start()

    def last(self):
        for p in (0, 1):
            self.arrive(self.slab(p, 2, 0), p, 6)
            self.arrive(self.slab(p, 2, 1), p, 7)
            self.copy(self.slab(p, 2), p, 11, self.here.front(dc=1)).start()

    def finish(self):
        for p in (0, 1):
            for slot, db in ((8, 0), (9, 3), (10, 1), (11, 2)):
                self.arrive(self.slab(p, db, dc=1), p, slot)
        for p in (0, 1):
            for slot, ref in (
                (0, self.block(p, 0)),
                (1, self.block(p, 0)),
                (2, self.block(p, 3, 0)),
                (3, self.block(p, 1, 1)),
                (4, self.slab(p, 0)),
                (5, self.slab(p, 0)),
                (6, self.slab(p, 3, 0)),
                (7, self.slab(p, 1, 1)),
                (8, self.slab(p, 0)),
                (9, self.slab(p, 3)),
                (10, self.slab(p, 1)),
                (11, self.slab(p, 2)),
            ):
                self.copy(ref, p, slot, self.here.front(dc=1)).wait_send()


def scaled(values, blocks, flags):
    pairs = blocks.shape[1]
    rows = 2 * pairs
    link = flags.astype(F32) * blocks[2:3]
    table = jnp.concatenate([blocks[0:2], link, jnp.zeros((5, pairs), F32)], axis=0)
    spread = (
        lax.broadcasted_iota(jnp.int32, (pairs, rows), 0)
        == lax.shift_right_logical(lax.broadcasted_iota(jnp.int32, (pairs, rows), 1), 1)
    ).astype(F32)
    wide = jnp.dot(table, spread, precision=lax.Precision.HIGHEST, preferred_element_type=F32)
    down = lax.broadcasted_iota(jnp.int32, (rows, rows), 0)
    over = lax.broadcasted_iota(jnp.int32, (rows, rows), 1)
    odd = lax.broadcasted_iota(jnp.int32, (1, rows), 1) & 1
    main = jnp.where(odd == 0, wide[0:1], wide[1:2])
    matrix = jnp.where(down == over, main, jnp.where((down ^ 1) == over, wide[2:3], 0.0))
    return jnp.dot(
        matrix, values.astype(F32), precision=lax.Precision.HIGHEST, preferred_element_type=F32
    )


def contract_rows(left, right):
    return lax.dot_general(left, right, (((0,), (0,)), ((), ())), preferred_element_type=F32)


def kernel(
    inverse_root, values_root, blocks_root, pairs_root,
    inverse_mid, lower_mid, values_mid, blocks_mid, pairs_mid, rows_mid,
    inverse_low, lower_low, lower_delay, values_low, blocks_low, pairs_low, rows_low, delayed_low,
    out_root, out_mid, out_low,
    ga, gb, gc, v_inv_root, v_inv_mid, v_lower_mid, v_lower_low, v_low, scaled_low,
    floats, stage, picked, root_picks, low_picks, reduced, part_send, part_recv,
    send, recv, y_send, y_recv, load_sem, inv_sem, out_sem,
):
    here = Here()
    z, x, c = here.z, here.x, here.c
    loads = [
        pltpu.make_async_copy(inverse_root, v_inv_root, load_sem.at[0]),
        pltpu.make_async_copy(lower_mid.at[0], v_lower_mid, load_sem.at[1]),
        pltpu.make_async_copy(inverse_mid.at[0], v_inv_mid, load_sem.at[2]),
        pltpu.make_async_copy(values_low.at[0], v_low, load_sem.at[3]),
        pltpu.make_async_copy(lower_low.at[0], v_lower_low.at[pl.ds(0, PICK)], load_sem.at[4]),
        pltpu.make_async_copy(lower_delay.at[0], v_lower_low.at[pl.ds(PICK, DELAY)], load_sem.at[5]),
    ]
    for load in loads:
        load.start()

    barrier = pltpu.get_barrier_semaphore()
    partners = [
        here.front(dx=1), here.front(dx=3), here.front(dz=1), here.front(dz=3), here.front(dc=1),
        here.level(1), here.level(2), here.level(3),
    ]
    for partner in partners:
        pl.semaphore_signal(barrier, inc=1, device_id=partner, device_id_type=MESH)
    whole_root = scaled(values_root[...], blocks_root[...], pairs_root[...]).astype(BF16)
    pl.semaphore_wait(barrier, len(partners))

    def level_copy(src, dst, h, slot, d):
        return pltpu.make_async_remote_copy(
            src_ref=src, dst_ref=dst, send_sem=y_send.at[h, slot], recv_sem=y_recv.at[h, slot],
            device_id=here.level(d), device_id_type=MESH,
        )

    def gather(buf, h, which, parts):
        return PlaneGather(here, buf, send.at[h, which], recv.at[h, which], parts)

    def inverse_low_copy(h, i):
        zz, rr = lax.div(i, 8), lax.rem(i, 8)
        return pltpu.make_async_copy(
            inverse_low.at[
                0,
                pl.ds(pl.multiple_of(rr * 256, 256), 256),
                pl.ds(pl.multiple_of((h * 4 + zz) * 256, 256), 256),
            ],
            gc.at[h, zz, lax.div(rr, 2), lax.rem(rr, 2)],
            inv_sem.at[h, i],
        )

    def sweep(h):
        cols = pl.ds(h * WIDE, WIDE)
        ga[h, z, x, c] = whole_root[:, h * WIDE:(h + 1) * WIDE]
        step = gather(ga.at[h], h, 0, ((0, 32, 16), (48, 16, 32)))
        step.begin()
        yield
        step.hop2()
        yield
        step.hop3()
        yield
        step.hop4()
        yield
        step.last()
        yield
        step.finish()
        if h == 0:
            loads[0].wait()
        total = jnp.zeros((384, WIDE), F32)
        for zz in range(4):
            total = total + jnp.dot(
                v_inv_root[:, zz * 768:(zz + 1) * 768],
                ga[h, zz].reshape(768, WIDE),
                preferred_element_type=F32,
            )
        part_send[h] = total.reshape(4, 96, WIDE)
        for d in (1, 2, 3):
            level_copy(
                part_send.at[h, lax.rem(here.y + d, 4)], part_recv.at[h, d - 1], h, d - 1, d
            ).start()
        yield
        for d in (1, 2, 3):
            level_copy(part_send.at[h, here.y], part_recv.at[h, d - 1], h, d - 1, d).wait_recv()
        own = part_send[h, here.y]
        for d in (1, 2, 3):
            own = own + part_recv[h, d - 1]
        own = own.astype(BF16)
        mine = pl.ds(pl.multiple_of(here.y * 96, 96), 96)
        gb[h, z, x, c, mine, :] = own
        for d in (1, 2, 3):
            place = gb.at[h, z, x, c, mine]
            level_copy(place, place, h, 2 + d, d).start()
        yield
        for d in (1, 2, 3):
            theirs = pl.ds(pl.multiple_of(lax.rem(here.y + 4 - d, 4) * 96, 96), 96)
            place = gb.at[h, z, x, c, theirs]
            level_copy(place, place, h, 2 + d, d).wait_recv()
        step = gather(gb.at[h], h, 1, ((0, 96, 96), (192, 96, 96)))
        step.begin()
        for d in (1, 2, 3):
            level_copy(part_send.at[h, here.y], part_recv.at[h, d - 1], h, d - 1, d).wait_send()
            place = gb.at[h, z, x, c, mine]
            level_copy(place, place, h, 2 + d, d).wait_send()
        yield
        step.hop2()
        yield
        step.hop3()
        yield
        step.hop4()
        yield
        step.last()
        yield
        step.finish()
        out_root[:, h * WIDE:(h + 1) * WIDE] = gb[
            h, here.y, z, lax.div(x, 2), pl.ds(pl.multiple_of((lax.rem(x, 2) * 2 + c) * 96, 96), 96), :
        ]
        for q in range(QUARTERS):
            lanes = slice(q * 128, (q + 1) * 128)

            @pl.loop(0, 32)
            def _(i):
                floats[pl.ds(pl.multiple_of(i * 384, 384), 384), :] = gb[
                    h, lax.div(i, 8), lax.rem(lax.div(i, 2), 4), lax.rem(i, 2), :, lanes
                ].astype(F32)

            @pl.loop(0, UPD // 512)
            def _(j):
                @pl.loop(0, 32)
                def _(i):
                    for k in range(16):
                        stage[pl.ds(i * 16 + k, 1), :] = floats[
                            pl.ds(rows_mid[0, j * 512 + i * 16 + k], 1), :
                        ]

                picked[pl.ds(pl.multiple_of(j * 512, 512), 512), lanes] = stage[0:512, :].astype(BF16)

            @pl.loop(0, PICK // 16)
            def _(i):
                for k in range(16):
                    u = i * 16 + k
                    root_picks[h, q, pl.ds(u, 1), :] = floats[
                        pl.ds(jnp.minimum(rows_low[0, u], ROOT - 1), 1), :
                    ]

            yield
        if h == 0:
            loads[1].wait()
        update = contract_rows(v_lower_mid[...], picked[...])
        ready = scaled(values_mid[0, :, h * WIDE:(h + 1) * WIDE], blocks_mid[0], pairs_mid[...])
        gc[h, z, x, c] = (ready - update).astype(BF16)
        step = gather(gc.at[h], h, 2, ((0, 64, 64), (128, 64, 64)))
        step.begin()
        yield
        step.hop2()
        yield
        step.hop3()
        yield
        step.hop4()
        yield
        step.last()
        yield
        step.finish()
        if h == 0:
            loads[2].wait()
        total = jnp.zeros((256, WIDE), F32)
        for zz in range(4):
            total = total + jnp.dot(
                v_inv_mid[:, zz * 2048:(zz + 1) * 2048],
                gc[h, zz].reshape(2048, WIDE),
                preferred_element_type=F32,
            )
        total = total.astype(BF16)
        out_mid[0, :, h * WIDE:(h + 1) * WIDE] = total
        gb[h, z, x, c, 0:256, :] = total
        step = gather(gb.at[h], h, 3, ((0, 64, 64), (128, 64, 64)))
        step.begin()

        @pl.loop(0, 32)
        def _(i):
            inverse_low_copy(h, i).start()

        yield
        step.hop2()
        yield
        step.hop3()
        yield
        step.hop4()
        yield
        if h == 0:
            loads[3].wait()

            @pl.loop(0, LOW // 256)
            def _(i):
                some = pl.ds(pl.multiple_of(i * 256, 256), 256)
                pairs = pl.ds(pl.multiple_of(i * 128, 128), 128)
                scaled_low[some, :] = scaled(v_low[some, :], blocks_low[0, :, pairs], pairs_low[:, pairs])

        step.last()
        yield
        step.finish()
        for q in range(QUARTERS):
            lanes = slice(q * 128, (q + 1) * 128)

            @pl.loop(0, 32)
            def _(i):
                floats[pl.ds(pl.multiple_of(i * 256, 256), 256), :] = gb[
                    h, lax.div(i, 8), lax.rem(lax.div(i, 2), 4), lax.rem(i, 2), 0:256, lanes
                ].astype(F32)

            @pl.loop(0, PICK // 16)
            def _(i):
                for k in range(16):
                    u = i * 16 + k
                    row = rows_low[0, u]
                    below = floats[pl.ds(jnp.maximum(row - ROOT, 0), 1), :]
                    above = root_picks[h, q, pl.ds(u, 1), :]
                    stage[pl.ds(u, 1), :] = jnp.where(row < ROOT, above, below)

            @pl.loop(0, DELAY // 16)
            def _(i):
                for k in range(16):
                    u = i * 16 + k
                    stage[pl.ds(PICK + u, 1), :] = floats[pl.ds(delayed_low[0, u], 1), :]

            low_picks[:, lanes] = stage[...].astype(BF16)
        yield
        if h == 0:
            loads[4].wait()
            loads[5].wait()

        @pl.loop(0, LOW // 256)
        def _(i):
            some = pl.ds(pl.multiple_of(i * 256, 256), 256)
            update = contract_rows(v_lower_low[:, some], low_picks[...])
            reduced[some, :] = (scaled_low[some, cols] - update).astype(BF16)

        yield

    def finish_low(h, first, end):
        @pl.loop(first, end)
        def _(i):
            total = jnp.zeros((256, WIDE), F32)
            for k in range(8):
                total = total + jnp.dot(
                    gc[k // 4, k % 4, lax.div(i, 2), lax.rem(i, 2)],
                    reduced[k * 256:(k + 1) * 256, :],
                    preferred_element_type=F32,
                )
            v_low[pl.ds(pl.multiple_of(i * 256, 256), 256), h * WIDE:(h + 1) * WIDE] = total.astype(BF16)

    halves = [sweep(h) for h in range(HALVES)]
    steps = 5 + 2 + 5 + QUARTERS + 5 + 5 + 2
    lag = 6

    def run(h, count=1):
        for _ in range(count):
            next(halves[h])

    run(0, lag)
    for _ in range(steps - lag):
        run(1)
        run(0)
    for h in range(HALVES):

        @pl.loop(0, 32)
        def _(i):
            inverse_low_copy(h, i).wait()

    for i in range(4):
        finish_low(0, 2 * i, 2 * i + 2)
        run(1)
    run(1, lag - 4)
    finish_low(1, 0, 8)
    store = pltpu.make_async_copy(v_low, out_low.at[0], out_sem.at[0])
    store.start()
    store.wait()


def on_device(*args):
    args = list(args)
    args[3] = args[3].reshape(1, -1)
    hbm = pl.BlockSpec(memory_space=pl.ANY)
    vmem = pl.BlockSpec(memory_space=pltpu.VMEM)
    smem = pl.BlockSpec(memory_space=pltpu.SMEM)
    return pl.pallas_call(
        kernel,
        out_shape=(
            jax.ShapeDtypeStruct((96, 512), BF16),
            jax.ShapeDtypeStruct((1, 256, 512), BF16),
            jax.ShapeDtypeStruct((1, LOW, 512), BF16),
        ),
        in_specs=[
            hbm, vmem, vmem, vmem,
            hbm, hbm, vmem, vmem, vmem, smem,
            hbm, hbm, hbm, hbm, vmem, vmem, smem, smem,
        ],
        out_specs=(vmem, vmem, hbm),
        scratch_shapes=[
            pltpu.VMEM((HALVES, 4, 4, 2, 96, WIDE), BF16),
            pltpu.VMEM((HALVES, 4, 4, 2, 384, WIDE), BF16),
            pltpu.VMEM((HALVES, 4, 4, 2, 256, WIDE), BF16),
            pltpu.VMEM((384, 3072), BF16),
            pltpu.VMEM((256, MID), BF16),
            pltpu.VMEM((UPD, 256), BF16),
            pltpu.VMEM((PICK + DELAY, LOW), BF16),
            pltpu.VMEM((LOW, 512), BF16),
            pltpu.VMEM((LOW, 512), F32),
            pltpu.VMEM((ROOT, 128), F32),
            pltpu.VMEM((PICK + DELAY, 128), F32),
            pltpu.VMEM((UPD, WIDE), BF16),
            pltpu.VMEM((HALVES, QUARTERS, PICK, 128), F32),
            pltpu.VMEM((PICK + DELAY, WIDE), BF16),
            pltpu.VMEM((LOW, WIDE), BF16),
            pltpu.VMEM((HALVES, 4, 96, WIDE), F32),
            pltpu.VMEM((HALVES, 3, 96, WIDE), F32),
            pltpu.SemaphoreType.DMA((HALVES, GATHERS, SLOTS)),
            pltpu.SemaphoreType.DMA((HALVES, GATHERS, SLOTS)),
            pltpu.SemaphoreType.DMA((HALVES, 6)),
            pltpu.SemaphoreType.DMA((HALVES, 6)),
            pltpu.SemaphoreType.DMA((6,)),
            pltpu.SemaphoreType.DMA((2, 32)),
            pltpu.SemaphoreType.DMA((1,)),
        ],
        compiler_params=pltpu.CompilerParams(
            collective_id=0, has_side_effects=True, vmem_limit_bytes=63 * 1024 * 1024
        ),
    )(*args)


def solution(mesh):
    placed = (
        P("front", "subtree"),
        P(("subtree", "front"), None),
        P(None, ("subtree", "front")),
        P(("subtree", "front")),
        P("subtree", "front", None),
        P("subtree", None, "front"),
        P("subtree", "front", None),
        P("subtree", None, "front"),
        P("subtree", "front"),
        P("subtree", None),
        P(("subtree", "front"), None, None),
        P(("subtree", "front"), None, None),
        P(("subtree", "front"), None, None),
        P(("subtree", "front"), None, None),
        P(("subtree", "front"), None, None),
        P(("subtree", "front"), None),
        P(("subtree", "front"), None),
        P(("subtree", "front"), None),
    )
    return jax.shard_map(
        on_device,
        mesh=mesh,
        in_specs=placed,
        out_specs=(
            P(("subtree", "front"), None),
            P("subtree", "front", None),
            P(("subtree", "front"), None, None),
        ),
        check_vma=False,
    )
```

```python
import jax
import jax.numpy as jnp
from jax import lax
from jax.experimental import pallas as pl
from jax.experimental.pallas import tpu as pltpu
from jax.sharding import PartitionSpec as P

MESH = pl.DeviceIdType.MESH
F32, BF16 = jnp.float32, jnp.bfloat16
HALVES = 2
WIDE = 512 // HALVES
ROOT = 12288
MID = 8192
UPD = 4096
LOW = 2048
PICK = 1024
DELAY = 128
GATHERS = 7
SLOTS = 24


def front_of(z, x, c):
    return (lax.rem(z, 4) * 4 + lax.rem(x, 4)) * 2 + lax.rem(c, 2)


class Here:
    def __init__(self):
        self.y = lax.axis_index("subtree")
        f = lax.axis_index("front")
        self.z = lax.div(f, 8)
        self.x = lax.rem(lax.div(f, 2), 4)
        self.c = lax.rem(f, 2)

    def front(self, dz=0, dx=0, dc=0):
        return (self.y, front_of(self.z + dz, self.x + dx, self.c + dc))

    def level(self, dy):
        return (lax.rem(self.y + dy, 4), front_of(self.z, self.x, self.c))


class PlaneGather:
    def __init__(self, here, buf, send, recv, parts):
        self.here, self.buf, self.send, self.recv, self.parts = here, buf, send, recv, parts

    def rows(self, p, sub):
        start, first, second = self.parts[p]
        if sub is None:
            return pl.ds(start, first + second)
        return pl.ds(start, first) if sub == 0 else pl.ds(start + first, second)

    def block(self, p, da, sub=None):
        h = self.here
        if p == 0:
            return self.buf.at[h.z, lax.rem(h.x + da, 4), h.c, self.rows(p, sub)]
        return self.buf.at[lax.rem(h.z + da, 4), h.x, h.c, self.rows(p, sub)]

    def slab(self, p, db, sub=None, dc=0):
        h = self.here
        c = lax.rem(h.c + dc, 2)
        if p == 0:
            return self.buf.at[lax.rem(h.z + db, 4), :, c, self.rows(p, sub)]
        return self.buf.at[:, lax.rem(h.x + db, 4), c, self.rows(p, sub)]

    def along(self, p, step):
        return self.here.front(dx=step) if p == 0 else self.here.front(dz=step)

    def across(self, p, step):
        return self.here.front(dz=step) if p == 0 else self.here.front(dx=step)

    def copy(self, ref, p, slot, target):
        return pltpu.make_async_remote_copy(
            src_ref=ref,
            dst_ref=ref,
            send_sem=self.send.at[p * 12 + slot],
            recv_sem=self.recv.at[p * 12 + slot],
            device_id=target,
            device_id_type=MESH,
        )

    def arrive(self, ref, p, slot):
        self.copy(ref, p, slot, self.here.front(dc=1)).wait_recv()

    def begin(self):
        for p in (0, 1):
            self.copy(self.block(p, 0), p, 0, self.along(p, 1)).start()
            self.copy(self.block(p, 0), p, 1, self.along(p, 3)).start()

    def hop2(self):
        for p in (0, 1):
            self.arrive(self.block(p, 3), p, 0)
            self.copy(self.block(p, 3, 0), p, 2, self.along(p, 1)).start()
            self.arrive(self.block(p, 1), p, 1)
            self.copy(self.block(p, 1, 1), p, 3, self.along(p, 3)).start()

    def hop3(self):
        for p in (0, 1):
            self.arrive(self.block(p, 2, 0), p, 2)
            self.arrive(self.block(p, 2, 1), p, 3)
            self.copy(self.slab(p, 0), p, 4, self.across(p, 1)).start()
            self.copy(self.slab(p, 0), p, 5, self.across(p, 3)).start()
        for p in (0, 1):
            self.copy(self.slab(p, 0), p, 8, self.here.front(dc=1)).start()

    def hop4(self):
        for p in (0, 1):
            self.arrive(self.slab(p, 3), p, 4)
            self.copy(self.slab(p, 3, 0), p, 6, self.across(p, 1)).start()
            self.arrive(self.slab(p, 1), p, 5)
            self.copy(self.slab(p, 1, 1), p, 7, self.across(p, 3)).start()
        for p in (0, 1):
            self.copy(self.slab(p, 3), p, 9, self.here.front(dc=1)).start()
            self.copy(self.slab(p, 1), p, 10, self.here.front(dc=1)).start()

    def last(self):
        for p in (0, 1):
            self.arrive(self.slab(p, 2, 0), p, 6)
            self.arrive(self.slab(p, 2, 1), p, 7)
            self.copy(self.slab(p, 2), p, 11, self.here.front(dc=1)).start()

    def finish(self):
        for p in (0, 1):
            for slot, db in ((8, 0), (9, 3), (10, 1), (11, 2)):
                self.arrive(self.slab(p, db, dc=1), p, slot)
        for p in (0, 1):
            for slot, ref in (
                (0, self.block(p, 0)),
                (1, self.block(p, 0)),
                (2, self.block(p, 3, 0)),
                (3, self.block(p, 1, 1)),
                (4, self.slab(p, 0)),
                (5, self.slab(p, 0)),
                (6, self.slab(p, 3, 0)),
                (7, self.slab(p, 1, 1)),
                (8, self.slab(p, 0)),
                (9, self.slab(p, 3)),
                (10, self.slab(p, 1)),
                (11, self.slab(p, 2)),
            ):
                self.copy(ref, p, slot, self.here.front(dc=1)).wait_send()


def scaled(values, first, second, coupling, flags):
    pairs = flags.shape[1]
    rows = 2 * pairs
    link = flags.astype(F32) * coupling
    table = jnp.concatenate([first, second, link, jnp.zeros((5, pairs), F32)], axis=0)
    spread = (
        lax.broadcasted_iota(jnp.int32, (pairs, rows), 0)
        == lax.shift_right_logical(lax.broadcasted_iota(jnp.int32, (pairs, rows), 1), 1)
    ).astype(F32)
    wide = jnp.dot(table, spread, precision=lax.Precision.HIGHEST, preferred_element_type=F32)
    down = lax.broadcasted_iota(jnp.int32, (rows, rows), 0)
    over = lax.broadcasted_iota(jnp.int32, (rows, rows), 1)
    odd = lax.broadcasted_iota(jnp.int32, (1, rows), 1) & 1
    main = jnp.where(odd == 0, wide[0:1], wide[1:2])
    matrix = jnp.where(down == over, main, jnp.where((down ^ 1) == over, wide[2:3], 0.0))
    return jnp.dot(
        matrix, values.astype(F32), precision=lax.Precision.HIGHEST, preferred_element_type=F32
    )


def contract_rows(left, right):
    return lax.dot_general(left, right, (((0,), (0,)), ((), ())), preferred_element_type=F32)


def kernel(
    inverse_root, values_root, blocks_root, pairs_root,
    inverse_mid, lower_mid, values_mid, blocks_mid, pairs_mid, rows_mid,
    lower_low, lower_delay, values_low, blocks_low, pairs_low, rows_low, delayed_low,
    out_root, out_mid, out_reduced,
    ga, gb, gc, v_inv_root, v_inv_mid, v_lower_mid, v_lower_low, v_low, scaled_low, scaled_mid,
    floats, stage, picked, low_picks, part_send, part_recv,
    send, recv, y_send, y_recv, load_sem,
):
    here = Here()
    z, x, c = here.z, here.x, here.c
    root_picks = v_low.at[pl.ds(0, PICK)]
    loads = [
        pltpu.make_async_copy(inverse_root, v_inv_root, load_sem.at[0]),
        pltpu.make_async_copy(lower_mid.at[0], v_lower_mid, load_sem.at[1]),
        pltpu.make_async_copy(inverse_mid.at[0], v_inv_mid, load_sem.at[2]),
        pltpu.make_async_copy(values_low.at[0], v_low, load_sem.at[3]),
        pltpu.make_async_copy(lower_low.at[0], v_lower_low.at[pl.ds(0, PICK)], load_sem.at[4]),
        pltpu.make_async_copy(lower_delay.at[0], v_lower_low.at[pl.ds(PICK, DELAY)], load_sem.at[5]),
    ]
    barrier = pltpu.get_barrier_semaphore()
    partners = [
        here.front(dx=1), here.front(dx=3), here.front(dz=1), here.front(dz=3), here.front(dc=1),
        here.level(1), here.level(2), here.level(3),
    ]
    for partner in partners:
        pl.semaphore_signal(barrier, inc=1, device_id=partner, device_id_type=MESH)
    loads[0].start()
    ga[z, x, c] = scaled(
        values_root[...], blocks_root[0:1, :], blocks_root[1:2, :], blocks_root[2:3, :], pairs_root[...]
    ).astype(BF16)
    pl.semaphore_wait(barrier, len(partners))

    def level_copy(src, dst, slot, d):
        return pltpu.make_async_remote_copy(
            src_ref=src, dst_ref=dst, send_sem=y_send.at[slot], recv_sem=y_recv.at[slot],
            device_id=here.level(d), device_id_type=MESH,
        )

    def gather(buf, which, parts):
        return PlaneGather(here, buf, send.at[which], recv.at[which], parts)

    def scale_low(first, end):
        @pl.loop(first, end)
        def _(i):
            some = pl.ds(pl.multiple_of(i * 256, 256), 256)
            pairs = pl.ds(pl.multiple_of(i * 128, 128), 128)
            scaled_low[some, :] = scaled(
                v_low[some, :], blocks_low[0, :, pairs], blocks_low[1, :, pairs],
                blocks_low[2, :, pairs], pairs_low[:, pairs],
            )

    def to_floats(h, rows):
        @pl.loop(0, 32)
        def _(i):
            some = pl.ds(pl.multiple_of(i * rows, rows), rows)
            for q in range(2):
                floats[q, some, :] = gb[
                    h, lax.div(i, 8), lax.rem(lax.div(i, 2), 4), lax.rem(i, 2), 0:rows,
                    q * 128:(q + 1) * 128,
                ].astype(F32)

    step = gather(ga, 6, ((0, 32, 16), (48, 16, 32)))
    step.begin()
    step.hop2()
    step.hop3()
    step.hop4()
    step.last()
    step.finish()
    loads[0].wait()
    total = jnp.zeros((384, 512), F32)
    for zz in range(4):
        total = total + jnp.dot(
            v_inv_root[:, zz * 768:(zz + 1) * 768],
            ga[zz].reshape(768, 512),
            preferred_element_type=F32,
        )
    part_send[...] = total.astype(BF16).reshape(4, 96, 512)
    adds = [
        level_copy(part_send.at[lax.rem(here.y + d, 4)], part_recv.at[d - 1], d - 1, d) for d in (1, 2, 3)
    ]
    for copy in adds:
        copy.start()
    scaled_mid[...] = scaled(
        values_mid[0], blocks_mid[0], blocks_mid[1], blocks_mid[2], pairs_mid[...]
    )
    for copy in adds:
        copy.wait_recv()
    own = part_send[here.y].astype(F32)
    for d in (1, 2, 3):
        own = own + part_recv[d - 1].astype(F32)
    own = own.astype(BF16)
    mine = pl.ds(pl.multiple_of(here.y * 96, 96), 96)
    shares = []
    for h in range(HALVES):
        gb[h, z, x, c, mine, :] = own[:, h * WIDE:(h + 1) * WIDE]
        place = gb.at[h, z, x, c, mine]
        for d in (1, 2, 3):
            shares.append(level_copy(place, place, 3 * h + 2 + d, d))
            shares[-1].start()

    def sweep(h):
        cols = slice(h * WIDE, (h + 1) * WIDE)
        for d in (1, 2, 3):
            theirs = pl.ds(pl.multiple_of(lax.rem(here.y + 4 - d, 4) * 96, 96), 96)
            place = gb.at[h, z, x, c, theirs]
            level_copy(place, place, 3 * h + 2 + d, d).wait_recv()
        step = gather(gb.at[h], h, ((0, 96, 96), (192, 96, 96)))
        step.begin()
        if h == 0:
            for k in (3, 1, 2, 4, 5):
                loads[k].start()
        yield
        step.hop2()
        for copy in shares[3 * h:3 * h + 3]:
            copy.wait_send()
        if h == 1:
            loads[3].wait()
            scale_low(0, 3)
        yield
        step.hop3()
        if h == 1:
            scale_low(3, 6)
        yield
        step.hop4()
        if h == 1:
            scale_low(6, 8)
        yield
        step.last()
        yield
        step.finish()
        out_root[:, cols] = gb[
            h, here.y, z, lax.div(x, 2), pl.ds(pl.multiple_of((lax.rem(x, 2) * 2 + c) * 96, 96), 96), :
        ]
        to_floats(h, 384)
        for part in range(2):

            @pl.loop(part * (UPD // 1024), (part + 1) * (UPD // 1024))
            def _(j):
                @pl.loop(0, 8)
                def _(i):
                    for k in range(64):
                        row = rows_mid[0, j * 512 + i * 64 + k]
                        for q in range(2):
                            stage[q, pl.ds(i * 64 + k, 1), :] = floats[q, pl.ds(row, 1), :]

                some = pl.ds(pl.multiple_of(j * 512, 512), 512)
                for q in range(2):
                    picked[some, q * 128:(q + 1) * 128] = stage[q, 0:512, :].astype(BF16)

            yield
        if h == 0:
            loads[1].wait()
        gc[h, z, x, c] = (
            scaled_mid[:, cols] - contract_rows(v_lower_mid[...], picked[...])
        ).astype(BF16)
        quarters = ((0, 64, 64), (128, 64, 64))
        step = gather(gc.at[h], 2 + h, quarters)
        step.begin()

        @pl.loop(0, PICK // 64)
        def _(i):
            for k in range(64):
                u = i * 64 + k
                row = rows_low[0, u]
                above = jnp.minimum(row, ROOT - 1)
                for q in range(2):
                    stage[q, pl.ds(u, 1), :] = jnp.where(row < ROOT, floats[q, pl.ds(above, 1), :], 0.0)

        for q in range(2):
            root_picks[:, h * WIDE + q * 128:h * WIDE + (q + 1) * 128] = stage[q, 0:PICK, :].astype(BF16)
        yield
        step.hop2()
        yield
        step.hop3()
        yield
        step.hop4()
        yield
        step.last()
        yield
        step.finish()
        if h == 0:
            loads[2].wait()
        total = jnp.zeros((256, WIDE), F32)
        for zz in range(4):
            total = total + jnp.dot(
                v_inv_mid[:, zz * 2048:(zz + 1) * 2048],
                gc[h, zz].reshape(2048, WIDE),
                preferred_element_type=F32,
            )
        total = total.astype(BF16)
        gb[h, z, x, c, 0:256, :] = total
        step = gather(gb.at[h], 4 + h, quarters)
        step.begin()
        out_mid[0, :, cols] = total
        yield
        step.hop2()
        yield
        step.hop3()
        yield
        step.hop4()
        yield
        step.last()
        yield
        step.finish()
        to_floats(h, 256)

        @pl.loop(0, PICK // 64)
        def _(i):
            for k in range(64):
                u = i * 64 + k
                row = rows_low[0, u]
                below = jnp.maximum(row - ROOT, 0)
                for q in range(2):
                    stage[q, pl.ds(u, 1), :] = jnp.where(row < ROOT, 0.0, floats[q, pl.ds(below, 1), :])

        @pl.loop(0, DELAY // 64)
        def _(i):
            for k in range(64):
                u = i * 64 + k
                row = delayed_low[0, u]
                for q in range(2):
                    stage[q, pl.ds(PICK + u, 1), :] = floats[q, pl.ds(row, 1), :]

        for q in range(2):
            lanes = slice(q * 128, (q + 1) * 128)
            both = stage[q, 0:PICK, :] + root_picks[:, h * WIDE + q * 128:h * WIDE + (q + 1) * 128].astype(F32)
            low_picks[0:PICK, lanes] = both.astype(BF16)
            low_picks[PICK:PICK + DELAY, lanes] = stage[q, PICK:PICK + DELAY, :].astype(BF16)
        yield
        if h == 0:
            loads[4].wait()
            loads[5].wait()

        @pl.loop(0, LOW // 256)
        def _(i):
            some = pl.ds(pl.multiple_of(i * 256, 256), 256)
            update = contract_rows(v_lower_low[:, some], low_picks[...])
            out_reduced[some, cols] = (scaled_low[some, cols] - update).astype(BF16)

        yield

    halves = [sweep(h) for h in range(HALVES)]
    order = "01010101001001010101010101010101010111"
    for h in order:
        next(halves[int(h)])
    for copy in adds:
        copy.wait_send()


def last_product(inverse, reduced, root, mid, out_root, out_mid, out_low):
    @pl.when(pl.program_id(0) == 0)
    def _():
        out_root[...] = root[...]
        out_mid[...] = mid[...]

    out_low[0] = jnp.dot(inverse[0], reduced[...], preferred_element_type=F32).astype(BF16)


def on_device(
    inverse_root, values_root, blocks_root, pairs_root,
    inverse_mid, lower_mid, values_mid, blocks_mid, pairs_mid, rows_mid,
    inverse_low, lower_low, lower_delay, values_low, blocks_low, pairs_low, rows_low, delayed_low,
):
    hbm = pl.BlockSpec(memory_space=pl.ANY)
    vmem = pl.BlockSpec(memory_space=pltpu.VMEM)
    smem = pl.BlockSpec(memory_space=pltpu.SMEM)
    solved_root, solved_mid, reduced_low = pl.pallas_call(
        kernel,
        out_shape=(
            jax.ShapeDtypeStruct((96, 512), BF16),
            jax.ShapeDtypeStruct((1, 256, 512), BF16),
            jax.ShapeDtypeStruct((LOW, 512), BF16),
        ),
        in_specs=[
            hbm, vmem, vmem, vmem,
            hbm, hbm, vmem, vmem, vmem, smem,
            hbm, hbm, hbm, vmem, vmem, smem, smem,
        ],
        out_specs=(vmem, vmem, vmem),
        scratch_shapes=[
            pltpu.VMEM((4, 4, 2, 96, 512), BF16),
            pltpu.VMEM((HALVES, 4, 4, 2, 384, WIDE), BF16),
            pltpu.VMEM((HALVES, 4, 4, 2, 256, WIDE), BF16),
            pltpu.VMEM((384, 3072), BF16),
            pltpu.VMEM((256, MID), BF16),
            pltpu.VMEM((UPD, 256), BF16),
            pltpu.VMEM((PICK + DELAY, LOW), BF16),
            pltpu.VMEM((LOW, 512), BF16),
            pltpu.VMEM((LOW, 512), F32),
            pltpu.VMEM((256, 512), F32),
            pltpu.VMEM((2, ROOT, 128), F32),
            pltpu.VMEM((2, PICK + DELAY, 128), F32),
            pltpu.VMEM((UPD, WIDE), BF16),
            pltpu.VMEM((PICK + DELAY, WIDE), BF16),
            pltpu.VMEM((4, 96, 512), BF16),
            pltpu.VMEM((3, 96, 512), BF16),
            pltpu.SemaphoreType.DMA((GATHERS, SLOTS)),
            pltpu.SemaphoreType.DMA((GATHERS, SLOTS)),
            pltpu.SemaphoreType.DMA((9,)),
            pltpu.SemaphoreType.DMA((9,)),
            pltpu.SemaphoreType.DMA((6,)),
        ],
        compiler_params=pltpu.CompilerParams(
            collective_id=0, has_side_effects=True, vmem_limit_bytes=65400 * 1024
        ),
    )(
        inverse_root, values_root, blocks_root, pairs_root.reshape(1, -1),
        inverse_mid, lower_mid, values_mid, jnp.transpose(blocks_mid, (1, 0, 2)), pairs_mid, rows_mid,
        lower_low, lower_delay, values_low, jnp.transpose(blocks_low, (1, 0, 2)), pairs_low,
        rows_low, delayed_low,
    )
    some = 512
    return pl.pallas_call(
        last_product,
        grid=(LOW // some,),
        out_shape=(
            jax.ShapeDtypeStruct((96, 512), BF16),
            jax.ShapeDtypeStruct((1, 256, 512), BF16),
            jax.ShapeDtypeStruct((1, LOW, 512), BF16),
        ),
        in_specs=[
            pl.BlockSpec((1, some, LOW), lambda i: (0, i, 0)),
            pl.BlockSpec((LOW, 512), lambda i: (0, 0)),
            pl.BlockSpec((96, 512), lambda i: (0, 0)),
            pl.BlockSpec((1, 256, 512), lambda i: (0, 0, 0)),
        ],
        out_specs=(
            pl.BlockSpec((96, 512), lambda i: (0, 0)),
            pl.BlockSpec((1, 256, 512), lambda i: (0, 0, 0)),
            pl.BlockSpec((1, some, 512), lambda i: (0, i, 0)),
        ),
        compiler_params=pltpu.CompilerParams(vmem_limit_bytes=65400 * 1024),
    )(inverse_low, reduced_low, solved_root, solved_mid)


def solution(mesh):
    placed = (
        P("front", "subtree"),
        P(("subtree", "front"), None),
        P(None, ("subtree", "front")),
        P(("subtree", "front")),
        P("subtree", "front", None),
        P("subtree", None, "front"),
        P("subtree", "front", None),
        P("subtree", None, "front"),
        P("subtree", "front"),
        P("subtree", None),
        P(("subtree", "front"), None, None),
        P(("subtree", "front"), None, None),
        P(("subtree", "front"), None, None),
        P(("subtree", "front"), None, None),
        P(("subtree", "front"), None, None),
        P(("subtree", "front"), None),
        P(("subtree", "front"), None),
        P(("subtree", "front"), None),
    )
    return jax.shard_map(
        on_device,
        mesh=mesh,
        in_specs=placed,
        out_specs=(
            P(("subtree", "front"), None),
            P("subtree", "front", None),
            P(("subtree", "front"), None, None),
        ),
        check_vma=False,
    )
```

```python
import jax
import jax.numpy as jnp
from jax import lax
from jax.experimental import pallas as pl
from jax.experimental.pallas import tpu as pltpu
from jax.sharding import PartitionSpec as P

MESH = pl.DeviceIdType.MESH
F32, BF16 = jnp.float32, jnp.bfloat16
HALVES = 2
WIDE = 512 // HALVES
ROOT = 12288
MID = 8192
UPD = 4096
LOW = 2048
PICK = 1024
DELAY = 128
GATHERS = 7
SLOTS = 24


def front_of(z, x, c):
    return (lax.rem(z, 4) * 4 + lax.rem(x, 4)) * 2 + lax.rem(c, 2)


class Here:
    def __init__(self):
        self.y = lax.axis_index("subtree")
        f = lax.axis_index("front")
        self.z = lax.div(f, 8)
        self.x = lax.rem(lax.div(f, 2), 4)
        self.c = lax.rem(f, 2)

    def front(self, dz=0, dx=0, dc=0):
        return (self.y, front_of(self.z + dz, self.x + dx, self.c + dc))

    def level(self, dy):
        return (lax.rem(self.y + dy, 4), front_of(self.z, self.x, self.c))


class PlaneGather:
    def __init__(self, here, buf, send, recv, parts):
        self.here, self.buf, self.send, self.recv, self.parts = here, buf, send, recv, parts

    def rows(self, p, sub):
        start, first, second = self.parts[p]
        if sub is None:
            return pl.ds(start, first + second)
        return pl.ds(start, first) if sub == 0 else pl.ds(start + first, second)

    def block(self, p, da, sub=None):
        h = self.here
        if p == 0:
            return self.buf.at[h.z, lax.rem(h.x + da, 4), h.c, self.rows(p, sub)]
        return self.buf.at[lax.rem(h.z + da, 4), h.x, h.c, self.rows(p, sub)]

    def slab(self, p, db, sub=None, dc=0):
        h = self.here
        c = lax.rem(h.c + dc, 2)
        if p == 0:
            return self.buf.at[lax.rem(h.z + db, 4), :, c, self.rows(p, sub)]
        return self.buf.at[:, lax.rem(h.x + db, 4), c, self.rows(p, sub)]

    def along(self, p, step):
        return self.here.front(dx=step) if p == 0 else self.here.front(dz=step)

    def across(self, p, step):
        return self.here.front(dz=step) if p == 0 else self.here.front(dx=step)

    def copy(self, ref, p, slot, target):
        return pltpu.make_async_remote_copy(
            src_ref=ref,
            dst_ref=ref,
            send_sem=self.send.at[p * 12 + slot],
            recv_sem=self.recv.at[p * 12 + slot],
            device_id=target,
            device_id_type=MESH,
        )

    def arrive(self, ref, p, slot):
        self.copy(ref, p, slot, self.here.front(dc=1)).wait_recv()

    def begin(self):
        for p in (0, 1):
            self.copy(self.block(p, 0), p, 0, self.along(p, 1)).start()
            self.copy(self.block(p, 0), p, 1, self.along(p, 3)).start()

    def hop2(self):
        for p in (0, 1):
            self.arrive(self.block(p, 3), p, 0)
            self.copy(self.block(p, 3, 0), p, 2, self.along(p, 1)).start()
            self.arrive(self.block(p, 1), p, 1)
            self.copy(self.block(p, 1, 1), p, 3, self.along(p, 3)).start()

    def hop3(self):
        for p in (0, 1):
            self.arrive(self.block(p, 2, 0), p, 2)
            self.arrive(self.block(p, 2, 1), p, 3)
            self.copy(self.slab(p, 0), p, 4, self.across(p, 1)).start()
            self.copy(self.slab(p, 0), p, 5, self.across(p, 3)).start()
        for p in (0, 1):
            self.copy(self.slab(p, 0), p, 8, self.here.front(dc=1)).start()

    def hop4(self):
        for p in (0, 1):
            self.arrive(self.slab(p, 3), p, 4)
            self.copy(self.slab(p, 3, 0), p, 6, self.across(p, 1)).start()
            self.arrive(self.slab(p, 1), p, 5)
            self.copy(self.slab(p, 1, 1), p, 7, self.across(p, 3)).start()
        for p in (0, 1):
            self.copy(self.slab(p, 3), p, 9, self.here.front(dc=1)).start()
            self.copy(self.slab(p, 1), p, 10, self.here.front(dc=1)).start()

    def last(self):
        for p in (0, 1):
            self.arrive(self.slab(p, 2, 0), p, 6)
            self.arrive(self.slab(p, 2, 1), p, 7)
            self.copy(self.slab(p, 2), p, 11, self.here.front(dc=1)).start()

    def finish(self):
        for p in (0, 1):
            for slot, db in ((8, 0), (9, 3), (10, 1), (11, 2)):
                self.arrive(self.slab(p, db, dc=1), p, slot)
        for p in (0, 1):
            for slot, ref in (
                (0, self.block(p, 0)),
                (1, self.block(p, 0)),
                (2, self.block(p, 3, 0)),
                (3, self.block(p, 1, 1)),
                (4, self.slab(p, 0)),
                (5, self.slab(p, 0)),
                (6, self.slab(p, 3, 0)),
                (7, self.slab(p, 1, 1)),
                (8, self.slab(p, 0)),
                (9, self.slab(p, 3)),
                (10, self.slab(p, 1)),
                (11, self.slab(p, 2)),
            ):
                self.copy(ref, p, slot, self.here.front(dc=1)).wait_send()


def scaled(values, first, second, coupling, flags):
    pairs = flags.shape[1]
    rows = 2 * pairs
    link = flags.astype(F32) * coupling
    table = jnp.concatenate([first, second, link, jnp.zeros((5, pairs), F32)], axis=0)
    spread = (
        lax.broadcasted_iota(jnp.int32, (pairs, rows), 0)
        == lax.shift_right_logical(lax.broadcasted_iota(jnp.int32, (pairs, rows), 1), 1)
    ).astype(F32)
    wide = jnp.dot(table, spread, precision=lax.Precision.HIGHEST, preferred_element_type=F32)
    down = lax.broadcasted_iota(jnp.int32, (rows, rows), 0)
    over = lax.broadcasted_iota(jnp.int32, (rows, rows), 1)
    odd = lax.broadcasted_iota(jnp.int32, (1, rows), 1) & 1
    main = jnp.where(odd == 0, wide[0:1], wide[1:2])
    matrix = jnp.where(down == over, main, jnp.where((down ^ 1) == over, wide[2:3], 0.0))
    return jnp.dot(
        matrix, values.astype(F32), precision=lax.Precision.HIGHEST, preferred_element_type=F32
    )


def contract_rows(left, right):
    return lax.dot_general(left, right, (((0,), (0,)), ((), ())), preferred_element_type=F32)


def kernel(
    inverse_root, values_root, blocks_root, pairs_root,
    inverse_mid, lower_mid, values_mid, blocks_mid, pairs_mid, rows_mid,
    lower_low, lower_delay, values_low, blocks_low, pairs_low, rows_low, delayed_low,
    out_root, out_mid, out_reduced,
    ga, gb, gc, v_inv_root, v_inv_mid, v_lower_mid, v_lower_low, v_low, scaled_low, scaled_mid,
    floats, stage, picked, low_picks, part_send, part_recv,
    send, recv, y_send, y_recv, load_sem,
):
    here = Here()
    z, x, c = here.z, here.x, here.c
    root_picks = v_low.at[pl.ds(0, PICK)]
    loads = [
        pltpu.make_async_copy(inverse_root, v_inv_root, load_sem.at[0]),
        pltpu.make_async_copy(lower_mid.at[0], v_lower_mid, load_sem.at[1]),
        pltpu.make_async_copy(inverse_mid.at[0], v_inv_mid, load_sem.at[2]),
        pltpu.make_async_copy(values_low.at[0], v_low, load_sem.at[3]),
        pltpu.make_async_copy(lower_low.at[0], v_lower_low.at[pl.ds(0, PICK)], load_sem.at[4]),
        pltpu.make_async_copy(lower_delay.at[0], v_lower_low.at[pl.ds(PICK, DELAY)], load_sem.at[5]),
    ]
    barrier = pltpu.get_barrier_semaphore()
    partners = [
        here.front(dx=1), here.front(dx=3), here.front(dz=1), here.front(dz=3), here.front(dc=1),
        here.level(1), here.level(2), here.level(3),
    ]
    for partner in partners:
        pl.semaphore_signal(barrier, inc=1, device_id=partner, device_id_type=MESH)
    loads[0].start()
    ga[z, x, c] = scaled(
        values_root[...], blocks_root[0:1, :], blocks_root[1:2, :], blocks_root[2:3, :], pairs_root[...]
    ).astype(BF16)
    pl.semaphore_wait(barrier, len(partners))

    def level_copy(src, dst, slot, d):
        return pltpu.make_async_remote_copy(
            src_ref=src, dst_ref=dst, send_sem=y_send.at[slot], recv_sem=y_recv.at[slot],
            device_id=here.level(d), device_id_type=MESH,
        )

    def gather(buf, which, parts):
        return PlaneGather(here, buf, send.at[which], recv.at[which], parts)

    def scale_low(first, end):
        @pl.loop(first, end)
        def _(i):
            some = pl.ds(pl.multiple_of(i * 256, 256), 256)
            pairs = pl.ds(pl.multiple_of(i * 128, 128), 128)
            scaled_low[some, :] = scaled(
                v_low[some, :], blocks_low[0, :, pairs], blocks_low[1, :, pairs],
                blocks_low[2, :, pairs], pairs_low[:, pairs],
            )

    def to_floats(h, rows):
        @pl.loop(0, 32)
        def _(i):
            some = pl.ds(pl.multiple_of(i * rows, rows), rows)
            for q in range(2):
                floats[q, some, :] = gb[
                    h, lax.div(i, 8), lax.rem(lax.div(i, 2), 4), lax.rem(i, 2), 0:rows,
                    q * 128:(q + 1) * 128,
                ].astype(F32)

    step = gather(ga, 6, ((0, 32, 16), (48, 16, 32)))
    step.begin()
    step.hop2()
    step.hop3()
    step.hop4()
    step.last()
    step.finish()
    loads[0].wait()
    mine = pl.ds(pl.multiple_of(here.y * 96, 96), 96)

    def sweep(h):
        cols = slice(h * WIDE, (h + 1) * WIDE)
        total = jnp.zeros((384, WIDE), F32)
        for zz in range(4):
            total = total + jnp.dot(
                v_inv_root[:, zz * 768:(zz + 1) * 768],
                ga[zz, :, :, :, cols].reshape(768, WIDE),
                preferred_element_type=F32,
            )
        part_send[h] = total.astype(BF16).reshape(4, 96, WIDE)
        adds = [
            level_copy(
                part_send.at[h, lax.rem(here.y + d, 4)], part_recv.at[h, d - 1], 3 * h + d - 1, d
            )
            for d in (1, 2, 3)
        ]
        for copy in adds:
            copy.start()
        yield
        if h == 0:
            scaled_mid[...] = scaled(
                values_mid[0], blocks_mid[0], blocks_mid[1], blocks_mid[2], pairs_mid[...]
            )
        for copy in adds:
            copy.wait_recv()
        own = part_send[h, here.y].astype(F32)
        for d in (1, 2, 3):
            own = own + part_recv[h, d - 1].astype(F32)
        gb[h, z, x, c, mine, :] = own.astype(BF16)
        place = gb.at[h, z, x, c, mine]
        shares = [level_copy(place, place, 3 * h + 5 + d, d) for d in (1, 2, 3)]
        for copy in shares:
            copy.start()
        yield
        for d in (1, 2, 3):
            theirs = pl.ds(pl.multiple_of(lax.rem(here.y + 4 - d, 4) * 96, 96), 96)
            place = gb.at[h, z, x, c, theirs]
            level_copy(place, place, 3 * h + 5 + d, d).wait_recv()
        step = gather(gb.at[h], h, ((0, 96, 96), (192, 96, 96)))
        step.begin()
        if h == 0:
            for k in (3, 1, 2, 4, 5):
                loads[k].start()
        yield
        step.hop2()
        for copy in adds + shares:
            copy.wait_send()
        if h == 1:
            loads[3].wait()
            scale_low(0, 3)
        yield
        step.hop3()
        if h == 1:
            scale_low(3, 6)
        yield
        step.hop4()
        if h == 1:
            scale_low(6, 8)
        yield
        step.last()
        yield
        step.finish()
        out_root[:, cols] = gb[
            h, here.y, z, lax.div(x, 2), pl.ds(pl.multiple_of((lax.rem(x, 2) * 2 + c) * 96, 96), 96), :
        ]
        to_floats(h, 384)
        yield
        for part in range(2):

            @pl.loop(part * (UPD // 1024), (part + 1) * (UPD // 1024))
            def _(j):
                @pl.loop(0, 8)
                def _(i):
                    for k in range(64):
                        row = rows_mid[0, j * 512 + i * 64 + k]
                        for q in range(2):
                            stage[q, pl.ds(i * 64 + k, 1), :] = floats[q, pl.ds(row, 1), :]

                some = pl.ds(pl.multiple_of(j * 512, 512), 512)
                for q in range(2):
                    picked[some, q * 128:(q + 1) * 128] = stage[q, 0:512, :].astype(BF16)

            yield
        if h == 0:
            loads[1].wait()
        gc[h, z, x, c] = (
            scaled_mid[:, cols] - contract_rows(v_lower_mid[...], picked[...])
        ).astype(BF16)
        quarters = ((0, 64, 64), (128, 64, 64))
        step = gather(gc.at[h], 2 + h, quarters)
        step.begin()

        @pl.loop(0, PICK // 64)
        def _(i):
            for k in range(64):
                u = i * 64 + k
                row = rows_low[0, u]
                above = jnp.minimum(row, ROOT - 1)
                for q in range(2):
                    stage[q, pl.ds(u, 1), :] = jnp.where(row < ROOT, floats[q, pl.ds(above, 1), :], 0.0)

        for q in range(2):
            root_picks[:, h * WIDE + q * 128:h * WIDE + (q + 1) * 128] = stage[q, 0:PICK, :].astype(BF16)
        yield
        step.hop2()
        yield
        step.hop3()
        yield
        step.hop4()
        yield
        step.last()
        yield
        step.finish()
        if h == 0:
            loads[2].wait()
        total = jnp.zeros((256, WIDE), F32)
        for zz in range(4):
            total = total + jnp.dot(
                v_inv_mid[:, zz * 2048:(zz + 1) * 2048],
                gc[h, zz].reshape(2048, WIDE),
                preferred_element_type=F32,
            )
        total = total.astype(BF16)
        gb[h, z, x, c, 0:256, :] = total
        step = gather(gb.at[h], 4 + h, quarters)
        step.begin()
        out_mid[0, :, cols] = total
        yield
        step.hop2()
        yield
        step.hop3()
        yield
        step.hop4()
        yield
        step.last()
        yield
        step.finish()
        to_floats(h, 256)

        @pl.loop(0, PICK // 64)
        def _(i):
            for k in range(64):
                u = i * 64 + k
                row = rows_low[0, u]
                below = jnp.maximum(row - ROOT, 0)
                for q in range(2):
                    stage[q, pl.ds(u, 1), :] = jnp.where(row < ROOT, 0.0, floats[q, pl.ds(below, 1), :])

        @pl.loop(0, DELAY // 64)
        def _(i):
            for k in range(64):
                u = i * 64 + k
                row = delayed_low[0, u]
                for q in range(2):
                    stage[q, pl.ds(PICK + u, 1), :] = floats[q, pl.ds(row, 1), :]

        for q in range(2):
            lanes = slice(q * 128, (q + 1) * 128)
            both = stage[q, 0:PICK, :] + root_picks[:, h * WIDE + q * 128:h * WIDE + (q + 1) * 128].astype(F32)
            low_picks[0:PICK, lanes] = both.astype(BF16)
            low_picks[PICK:PICK + DELAY, lanes] = stage[q, PICK:PICK + DELAY, :].astype(BF16)
        yield
        if h == 0:
            loads[4].wait()
            loads[5].wait()

        @pl.loop(0, LOW // 256)
        def _(i):
            some = pl.ds(pl.multiple_of(i * 256, 256), 256)
            update = contract_rows(v_lower_low[:, some], low_picks[...])
            out_reduced[some, cols] = (scaled_low[some, cols] - update).astype(BF16)

        yield

    halves = [sweep(h) for h in range(HALVES)]
    order = "01001010101001010010101101010101010101010111"
    for h in order:
        next(halves[int(h)])


def last_product(inverse, reduced, root, mid, out_root, out_mid, out_low):
    @pl.when(pl.program_id(0) == 0)
    def _():
        out_root[...] = root[...]
        out_mid[...] = mid[...]

    out_low[0] = jnp.dot(inverse[0], reduced[...], preferred_element_type=F32).astype(BF16)


def on_device(
    inverse_root, values_root, blocks_root, pairs_root,
    inverse_mid, lower_mid, values_mid, blocks_mid, pairs_mid, rows_mid,
    inverse_low, lower_low, lower_delay, values_low, blocks_low, pairs_low, rows_low, delayed_low,
):
    hbm = pl.BlockSpec(memory_space=pl.ANY)
    vmem = pl.BlockSpec(memory_space=pltpu.VMEM)
    smem = pl.BlockSpec(memory_space=pltpu.SMEM)
    solved_root, solved_mid, reduced_low = pl.pallas_call(
        kernel,
        out_shape=(
            jax.ShapeDtypeStruct((96, 512), BF16),
            jax.ShapeDtypeStruct((1, 256, 512), BF16),
            jax.ShapeDtypeStruct((LOW, 512), BF16),
        ),
        in_specs=[
            hbm, vmem, vmem, vmem,
            hbm, hbm, vmem, vmem, vmem, smem,
            hbm, hbm, hbm, vmem, vmem, smem, smem,
        ],
        out_specs=(vmem, vmem, vmem),
        scratch_shapes=[
            pltpu.VMEM((4, 4, 2, 96, 512), BF16),
            pltpu.VMEM((HALVES, 4, 4, 2, 384, WIDE), BF16),
            pltpu.VMEM((HALVES, 4, 4, 2, 256, WIDE), BF16),
            pltpu.VMEM((384, 3072), BF16),
            pltpu.VMEM((256, MID), BF16),
            pltpu.VMEM((UPD, 256), BF16),
            pltpu.VMEM((PICK + DELAY, LOW), BF16),
            pltpu.VMEM((LOW, 512), BF16),
            pltpu.VMEM((LOW, 512), F32),
            pltpu.VMEM((256, 512), F32),
            pltpu.VMEM((2, ROOT, 128), F32),
            pltpu.VMEM((2, PICK + DELAY, 128), F32),
            pltpu.VMEM((UPD, WIDE), BF16),
            pltpu.VMEM((PICK + DELAY, WIDE), BF16),
            pltpu.VMEM((HALVES, 4, 96, WIDE), BF16),
            pltpu.VMEM((HALVES, 3, 96, WIDE), BF16),
            pltpu.SemaphoreType.DMA((GATHERS, SLOTS)),
            pltpu.SemaphoreType.DMA((GATHERS, SLOTS)),
            pltpu.SemaphoreType.DMA((12,)),
            pltpu.SemaphoreType.DMA((12,)),
            pltpu.SemaphoreType.DMA((6,)),
        ],
        compiler_params=pltpu.CompilerParams(
            collective_id=0, has_side_effects=True, vmem_limit_bytes=65400 * 1024
        ),
    )(
        inverse_root, values_root, blocks_root, pairs_root.reshape(1, -1),
        inverse_mid, lower_mid, values_mid, jnp.transpose(blocks_mid, (1, 0, 2)), pairs_mid, rows_mid,
        lower_low, lower_delay, values_low, jnp.transpose(blocks_low, (1, 0, 2)), pairs_low,
        rows_low, delayed_low,
    )
    some = 512
    return pl.pallas_call(
        last_product,
        grid=(LOW // some,),
        out_shape=(
            jax.ShapeDtypeStruct((96, 512), BF16),
            jax.ShapeDtypeStruct((1, 256, 512), BF16),
            jax.ShapeDtypeStruct((1, LOW, 512), BF16),
        ),
        in_specs=[
            pl.BlockSpec((1, some, LOW), lambda i: (0, i, 0)),
            pl.BlockSpec((LOW, 512), lambda i: (0, 0)),
            pl.BlockSpec((96, 512), lambda i: (0, 0)),
            pl.BlockSpec((1, 256, 512), lambda i: (0, 0, 0)),
        ],
        out_specs=(
            pl.BlockSpec((96, 512), lambda i: (0, 0)),
            pl.BlockSpec((1, 256, 512), lambda i: (0, 0, 0)),
            pl.BlockSpec((1, some, 512), lambda i: (0, i, 0)),
        ),
        compiler_params=pltpu.CompilerParams(vmem_limit_bytes=65400 * 1024),
    )(inverse_low, reduced_low, solved_root, solved_mid)


def solution(mesh):
    placed = (
        P("front", "subtree"),
        P(("subtree", "front"), None),
        P(None, ("subtree", "front")),
        P(("subtree", "front")),
        P("subtree", "front", None),
        P("subtree", None, "front"),
        P("subtree", "front", None),
        P("subtree", None, "front"),
        P("subtree", "front"),
        P("subtree", None),
        P(("subtree", "front"), None, None),
        P(("subtree", "front"), None, None),
        P(("subtree", "front"), None, None),
        P(("subtree", "front"), None, None),
        P(("subtree", "front"), None, None),
        P(("subtree", "front"), None),
        P(("subtree", "front"), None),
        P(("subtree", "front"), None),
    )
    return jax.shard_map(
        on_device,
        mesh=mesh,
        in_specs=placed,
        out_specs=(
            P(("subtree", "front"), None),
            P("subtree", "front", None),
            P(("subtree", "front"), None, None),
        ),
        check_vma=False,
    )
```

```python
import jax
import jax.numpy as jnp
from jax import lax
from jax.experimental import pallas as pl
from jax.experimental.pallas import tpu as pltpu
from jax.sharding import PartitionSpec as P

MESH = pl.DeviceIdType.MESH
F32, BF16 = jnp.float32, jnp.bfloat16
HALVES = 2
WIDE = 512 // HALVES
ROOT = 12288
MID = 8192
UPD = 4096
LOW = 2048
PICK = 1024
DELAY = 128
GATHERS = 7
SLOTS = 24


def front_of(z, x, c):
    return (lax.rem(z, 4) * 4 + lax.rem(x, 4)) * 2 + lax.rem(c, 2)


class Here:
    def __init__(self):
        self.y = lax.axis_index("subtree")
        f = lax.axis_index("front")
        self.z = lax.div(f, 8)
        self.x = lax.rem(lax.div(f, 2), 4)
        self.c = lax.rem(f, 2)

    def front(self, dz=0, dx=0, dc=0):
        return (self.y, front_of(self.z + dz, self.x + dx, self.c + dc))

    def level(self, dy):
        return (lax.rem(self.y + dy, 4), front_of(self.z, self.x, self.c))


class PlaneGather:
    def __init__(self, here, buf, send, recv, parts):
        self.here, self.buf, self.send, self.recv, self.parts = here, buf, send, recv, parts

    def rows(self, p, sub):
        start, first, second = self.parts[p]
        if sub is None:
            return pl.ds(start, first + second)
        return pl.ds(start, first) if sub == 0 else pl.ds(start + first, second)

    def block(self, p, da, sub=None):
        h = self.here
        if p == 0:
            return self.buf.at[h.z, lax.rem(h.x + da, 4), h.c, self.rows(p, sub)]
        return self.buf.at[lax.rem(h.z + da, 4), h.x, h.c, self.rows(p, sub)]

    def slab(self, p, db, sub=None, dc=0):
        h = self.here
        c = lax.rem(h.c + dc, 2)
        if p == 0:
            return self.buf.at[lax.rem(h.z + db, 4), :, c, self.rows(p, sub)]
        return self.buf.at[:, lax.rem(h.x + db, 4), c, self.rows(p, sub)]

    def along(self, p, step):
        return self.here.front(dx=step) if p == 0 else self.here.front(dz=step)

    def across(self, p, step):
        return self.here.front(dz=step) if p == 0 else self.here.front(dx=step)

    def copy(self, ref, p, slot, target):
        return pltpu.make_async_remote_copy(
            src_ref=ref,
            dst_ref=ref,
            send_sem=self.send.at[p * 12 + slot],
            recv_sem=self.recv.at[p * 12 + slot],
            device_id=target,
            device_id_type=MESH,
        )

    def arrive(self, ref, p, slot):
        self.copy(ref, p, slot, self.here.front(dc=1)).wait_recv()

    def begin(self):
        for p in (0, 1):
            self.copy(self.block(p, 0), p, 0, self.along(p, 1)).start()
            self.copy(self.block(p, 0), p, 1, self.along(p, 3)).start()

    def hop2(self):
        for p in (0, 1):
            self.arrive(self.block(p, 3), p, 0)
            self.copy(self.block(p, 3, 0), p, 2, self.along(p, 1)).start()
            self.arrive(self.block(p, 1), p, 1)
            self.copy(self.block(p, 1, 1), p, 3, self.along(p, 3)).start()

    def hop3(self):
        for p in (0, 1):
            self.arrive(self.block(p, 2, 0), p, 2)
            self.arrive(self.block(p, 2, 1), p, 3)
            self.copy(self.slab(p, 0), p, 4, self.across(p, 1)).start()
            self.copy(self.slab(p, 0), p, 5, self.across(p, 3)).start()
        for p in (0, 1):
            self.copy(self.slab(p, 0), p, 8, self.here.front(dc=1)).start()

    def hop4(self):
        for p in (0, 1):
            self.arrive(self.slab(p, 3), p, 4)
            self.copy(self.slab(p, 3, 0), p, 6, self.across(p, 1)).start()
            self.arrive(self.slab(p, 1), p, 5)
            self.copy(self.slab(p, 1, 1), p, 7, self.across(p, 3)).start()
        for p in (0, 1):
            self.copy(self.slab(p, 3), p, 9, self.here.front(dc=1)).start()
            self.copy(self.slab(p, 1), p, 10, self.here.front(dc=1)).start()

    def last(self):
        for p in (0, 1):
            self.arrive(self.slab(p, 2, 0), p, 6)
            self.arrive(self.slab(p, 2, 1), p, 7)
            self.copy(self.slab(p, 2), p, 11, self.here.front(dc=1)).start()

    def finish(self):
        for p in (0, 1):
            for slot, db in ((8, 0), (9, 3), (10, 1), (11, 2)):
                self.arrive(self.slab(p, db, dc=1), p, slot)
        for p in (0, 1):
            for slot, ref in (
                (0, self.block(p, 0)),
                (1, self.block(p, 0)),
                (2, self.block(p, 3, 0)),
                (3, self.block(p, 1, 1)),
                (4, self.slab(p, 0)),
                (5, self.slab(p, 0)),
                (6, self.slab(p, 3, 0)),
                (7, self.slab(p, 1, 1)),
                (8, self.slab(p, 0)),
                (9, self.slab(p, 3)),
                (10, self.slab(p, 1)),
                (11, self.slab(p, 2)),
            ):
                self.copy(ref, p, slot, self.here.front(dc=1)).wait_send()


def scaled(values, first, second, coupling, flags):
    pairs = flags.shape[1]
    rows = 2 * pairs
    link = flags.astype(F32) * coupling
    table = jnp.concatenate([first, second, link, jnp.zeros((5, pairs), F32)], axis=0)
    spread = (
        lax.broadcasted_iota(jnp.int32, (pairs, rows), 0)
        == lax.shift_right_logical(lax.broadcasted_iota(jnp.int32, (pairs, rows), 1), 1)
    ).astype(F32)
    wide = jnp.dot(table, spread, precision=lax.Precision.HIGHEST, preferred_element_type=F32)
    down = lax.broadcasted_iota(jnp.int32, (rows, rows), 0)
    over = lax.broadcasted_iota(jnp.int32, (rows, rows), 1)
    odd = lax.broadcasted_iota(jnp.int32, (1, rows), 1) & 1
    main = jnp.where(odd == 0, wide[0:1], wide[1:2])
    matrix = jnp.where(down == over, main, jnp.where((down ^ 1) == over, wide[2:3], 0.0))
    return jnp.dot(
        matrix, values.astype(F32), precision=lax.Precision.HIGHEST, preferred_element_type=F32
    )


def contract_rows(left, right):
    return lax.dot_general(left, right, (((0,), (0,)), ((), ())), preferred_element_type=F32)


def kernel(
    inverse_root, values_root, blocks_root, pairs_root,
    inverse_mid, lower_mid, values_mid, blocks_mid, pairs_mid, rows_mid,
    lower_low, lower_delay, values_low, blocks_low, pairs_low, rows_low, delayed_low,
    out_root, out_mid, out_reduced,
    ga, gb, gc, v_inv_root, v_inv_mid, v_lower_mid, v_lower_low, v_low, scaled_low, scaled_mid,
    floats, stage, picked, low_picks, part_send, part_recv,
    send, recv, y_send, y_recv, load_sem,
):
    here = Here()
    z, x, c = here.z, here.x, here.c
    root_picks = v_low.at[pl.ds(0, PICK)]
    loads = [
        pltpu.make_async_copy(inverse_root, v_inv_root, load_sem.at[0]),
        pltpu.make_async_copy(lower_mid.at[0], v_lower_mid, load_sem.at[1]),
        pltpu.make_async_copy(inverse_mid.at[0], v_inv_mid, load_sem.at[2]),
        pltpu.make_async_copy(values_low.at[0], v_low, load_sem.at[3]),
        pltpu.make_async_copy(lower_low.at[0], v_lower_low.at[pl.ds(0, PICK)], load_sem.at[4]),
        pltpu.make_async_copy(lower_delay.at[0], v_lower_low.at[pl.ds(PICK, DELAY)], load_sem.at[5]),
    ]
    barrier = pltpu.get_barrier_semaphore()
    partners = [
        here.front(dx=1), here.front(dx=3), here.front(dz=1), here.front(dz=3), here.front(dc=1),
        here.level(1), here.level(2), here.level(3),
    ]
    for partner in partners:
        pl.semaphore_signal(barrier, inc=1, device_id=partner, device_id_type=MESH)
    loads[0].start()
    ga[z, x, c] = scaled(
        values_root[...], blocks_root[0:1, :], blocks_root[1:2, :], blocks_root[2:3, :], pairs_root[...]
    ).astype(BF16)
    pl.semaphore_wait(barrier, len(partners))

    def level_copy(src, dst, slot, d):
        return pltpu.make_async_remote_copy(
            src_ref=src, dst_ref=dst, send_sem=y_send.at[slot], recv_sem=y_recv.at[slot],
            device_id=here.level(d), device_id_type=MESH,
        )

    def gather(buf, which, parts):
        return PlaneGather(here, buf, send.at[which], recv.at[which], parts)

    def scale_low(first, end):
        @pl.loop(first, end)
        def _(i):
            some = pl.ds(pl.multiple_of(i * 256, 256), 256)
            pairs = pl.ds(pl.multiple_of(i * 128, 128), 128)
            scaled_low[some, :] = scaled(
                v_low[some, :], blocks_low[0, :, pairs], blocks_low[1, :, pairs],
                blocks_low[2, :, pairs], pairs_low[:, pairs],
            )

    def to_floats(h, rows):
        @pl.loop(0, 32)
        def _(i):
            some = pl.ds(pl.multiple_of(i * rows, rows), rows)
            for q in range(2):
                floats[q, some, :] = gb[
                    h, lax.div(i, 8), lax.rem(lax.div(i, 2), 4), lax.rem(i, 2), 0:rows,
                    q * 128:(q + 1) * 128,
                ].astype(F32)

    step = gather(ga, 6, ((0, 32, 16), (48, 16, 32)))
    step.begin()
    step.hop2()
    step.hop3()
    step.hop4()
    step.last()
    step.finish()
    loads[0].wait()
    mine = pl.ds(pl.multiple_of(here.y * 96, 96), 96)

    def sweep(h):
        cols = slice(h * WIDE, (h + 1) * WIDE)
        total = jnp.zeros((384, WIDE), F32)
        for zz in range(4):
            total = total + jnp.dot(
                v_inv_root[:, zz * 768:(zz + 1) * 768],
                ga[zz, :, :, :, cols].reshape(768, WIDE),
                preferred_element_type=F32,
            )
        part_send[h] = total.astype(BF16).reshape(4, 96, WIDE)
        adds = [
            level_copy(
                part_send.at[h, lax.rem(here.y + d, 4)], part_recv.at[h, d - 1], 3 * h + d - 1, d
            )
            for d in (1, 2, 3)
        ]
        for copy in adds:
            copy.start()
        yield
        if h == 0:
            scaled_mid[...] = scaled(
                values_mid[0], blocks_mid[0], blocks_mid[1], blocks_mid[2], pairs_mid[...]
            )
        for copy in adds:
            copy.wait_recv()
        own = part_send[h, here.y].astype(F32)
        for d in (1, 2, 3):
            own = own + part_recv[h, d - 1].astype(F32)
        gb[h, z, x, c, mine, :] = own.astype(BF16)
        place = gb.at[h, z, x, c, mine]
        shares = [level_copy(place, place, 3 * h + 5 + d, d) for d in (1, 2, 3)]
        for copy in shares:
            copy.start()
        yield
        for d in (1, 2, 3):
            theirs = pl.ds(pl.multiple_of(lax.rem(here.y + 4 - d, 4) * 96, 96), 96)
            place = gb.at[h, z, x, c, theirs]
            level_copy(place, place, 3 * h + 5 + d, d).wait_recv()
        step = gather(gb.at[h], h, ((0, 96, 96), (192, 96, 96)))
        step.begin()
        if h == 0:
            for k in (3, 1, 2, 4, 5):
                loads[k].start()
        yield
        step.hop2()
        for copy in adds + shares:
            copy.wait_send()
        if h == 1:
            loads[3].wait()
            scale_low(0, 3)
        yield
        step.hop3()
        if h == 1:
            scale_low(3, 6)
        yield
        step.hop4()
        if h == 1:
            scale_low(6, 8)
        yield
        step.last()
        yield
        step.finish()
        out_root[:, cols] = gb[
            h, here.y, z, lax.div(x, 2), pl.ds(pl.multiple_of((lax.rem(x, 2) * 2 + c) * 96, 96), 96), :
        ]
        to_floats(h, 384)
        yield
        for part in range(2):

            @pl.loop(part * (UPD // 1024), (part + 1) * (UPD // 1024))
            def _(j):
                @pl.loop(0, 8)
                def _(i):
                    for k in range(64):
                        row = rows_mid[0, j * 512 + i * 64 + k]
                        for q in range(2):
                            stage[q, pl.ds(i * 64 + k, 1), :] = floats[q, pl.ds(row, 1), :]

                some = pl.ds(pl.multiple_of(j * 512, 512), 512)
                for q in range(2):
                    picked[some, q * 128:(q + 1) * 128] = stage[q, 0:512, :].astype(BF16)

            yield
        if h == 0:
            loads[1].wait()
        gc[h, z, x, c] = (
            scaled_mid[:, cols] - contract_rows(v_lower_mid[...], picked[...])
        ).astype(BF16)
        quarters = ((0, 64, 64), (128, 64, 64))
        step = gather(gc.at[h], 2 + h, quarters)
        step.begin()

        @pl.loop(0, PICK // 64)
        def _(i):
            for k in range(64):
                u = i * 64 + k
                row = rows_low[0, u]
                above = jnp.minimum(row, ROOT - 1)
                for q in range(2):
                    stage[q, pl.ds(u, 1), :] = jnp.where(row < ROOT, floats[q, pl.ds(above, 1), :], 0.0)

        for q in range(2):
            root_picks[:, h * WIDE + q * 128:h * WIDE + (q + 1) * 128] = stage[q, 0:PICK, :].astype(BF16)
        yield
        step.hop2()
        yield
        step.hop3()
        yield
        step.hop4()
        yield
        step.last()
        yield
        step.finish()
        if h == 0:
            loads[2].wait()
        total = jnp.zeros((256, WIDE), F32)
        for zz in range(4):
            total = total + jnp.dot(
                v_inv_mid[:, zz * 2048:(zz + 1) * 2048],
                gc[h, zz].reshape(2048, WIDE),
                preferred_element_type=F32,
            )
        total = total.astype(BF16)
        gb[h, z, x, c, 0:256, :] = total
        step = gather(gb.at[h], 4 + h, quarters)
        step.begin()
        out_mid[0, :, cols] = total
        yield
        step.hop2()
        yield
        step.hop3()
        yield
        step.hop4()
        yield
        step.last()
        yield
        step.finish()
        to_floats(h, 256)

        @pl.loop(0, PICK // 64)
        def _(i):
            for k in range(64):
                u = i * 64 + k
                row = rows_low[0, u]
                below = jnp.maximum(row - ROOT, 0)
                for q in range(2):
                    stage[q, pl.ds(u, 1), :] = jnp.where(row < ROOT, 0.0, floats[q, pl.ds(below, 1), :])

        @pl.loop(0, DELAY // 64)
        def _(i):
            for k in range(64):
                u = i * 64 + k
                row = delayed_low[0, u]
                for q in range(2):
                    stage[q, pl.ds(PICK + u, 1), :] = floats[q, pl.ds(row, 1), :]

        for q in range(2):
            lanes = slice(q * 128, (q + 1) * 128)
            both = stage[q, 0:PICK, :] + root_picks[:, h * WIDE + q * 128:h * WIDE + (q + 1) * 128].astype(F32)
            low_picks[0:PICK, lanes] = both.astype(BF16)
            low_picks[PICK:PICK + DELAY, lanes] = stage[q, PICK:PICK + DELAY, :].astype(BF16)
        yield
        if h == 0:
            loads[4].wait()
            loads[5].wait()

        @pl.loop(0, LOW // 256)
        def _(i):
            some = pl.ds(pl.multiple_of(i * 256, 256), 256)
            update = contract_rows(v_lower_low[:, some], low_picks[...])
            out_reduced[some, cols] = (scaled_low[some, cols] - update).astype(BF16)

        yield

    halves = [sweep(h) for h in range(HALVES)]
    order = "01001010101000100110101101010101010101010111"
    for h in order:
        next(halves[int(h)])


def last_product(inverse, reduced, root, mid, out_root, out_mid, out_low):
    @pl.when(pl.program_id(0) == 0)
    def _():
        out_root[...] = root[...]
        out_mid[...] = mid[...]

    out_low[0] = jnp.dot(inverse[0], reduced[...], preferred_element_type=F32).astype(BF16)


def on_device(
    inverse_root, values_root, blocks_root, pairs_root,
    inverse_mid, lower_mid, values_mid, blocks_mid, pairs_mid, rows_mid,
    inverse_low, lower_low, lower_delay, values_low, blocks_low, pairs_low, rows_low, delayed_low,
):
    hbm = pl.BlockSpec(memory_space=pl.ANY)
    vmem = pl.BlockSpec(memory_space=pltpu.VMEM)
    smem = pl.BlockSpec(memory_space=pltpu.SMEM)
    solved_root, solved_mid, reduced_low = pl.pallas_call(
        kernel,
        out_shape=(
            jax.ShapeDtypeStruct((96, 512), BF16),
            jax.ShapeDtypeStruct((1, 256, 512), BF16),
            jax.ShapeDtypeStruct((LOW, 512), BF16),
        ),
        in_specs=[
            hbm, vmem, vmem, vmem,
            hbm, hbm, vmem, vmem, vmem, smem,
            hbm, hbm, hbm, vmem, vmem, smem, smem,
        ],
        out_specs=(vmem, vmem, vmem),
        scratch_shapes=[
            pltpu.VMEM((4, 4, 2, 96, 512), BF16),
            pltpu.VMEM((HALVES, 4, 4, 2, 384, WIDE), BF16),
            pltpu.VMEM((HALVES, 4, 4, 2, 256, WIDE), BF16),
            pltpu.VMEM((384, 3072), BF16),
            pltpu.VMEM((256, MID), BF16),
            pltpu.VMEM((UPD, 256), BF16),
            pltpu.VMEM((PICK + DELAY, LOW), BF16),
            pltpu.VMEM((LOW, 512), BF16),
            pltpu.VMEM((LOW, 512), F32),
            pltpu.VMEM((256, 512), F32),
            pltpu.VMEM((2, ROOT, 128), F32),
            pltpu.VMEM((2, PICK + DELAY, 128), F32),
            pltpu.VMEM((UPD, WIDE), BF16),
            pltpu.VMEM((PICK + DELAY, WIDE), BF16),
            pltpu.VMEM((HALVES, 4, 96, WIDE), BF16),
            pltpu.VMEM((HALVES, 3, 96, WIDE), BF16),
            pltpu.SemaphoreType.DMA((GATHERS, SLOTS)),
            pltpu.SemaphoreType.DMA((GATHERS, SLOTS)),
            pltpu.SemaphoreType.DMA((12,)),
            pltpu.SemaphoreType.DMA((12,)),
            pltpu.SemaphoreType.DMA((6,)),
        ],
        compiler_params=pltpu.CompilerParams(
            collective_id=0, has_side_effects=True, vmem_limit_bytes=65400 * 1024
        ),
    )(
        inverse_root, values_root, blocks_root, pairs_root.reshape(1, -1),
        inverse_mid, lower_mid, values_mid, jnp.transpose(blocks_mid, (1, 0, 2)), pairs_mid, rows_mid,
        lower_low, lower_delay, values_low, jnp.transpose(blocks_low, (1, 0, 2)), pairs_low,
        rows_low, delayed_low,
    )
    some = 512
    return pl.pallas_call(
        last_product,
        grid=(LOW // some,),
        out_shape=(
            jax.ShapeDtypeStruct((96, 512), BF16),
            jax.ShapeDtypeStruct((1, 256, 512), BF16),
            jax.ShapeDtypeStruct((1, LOW, 512), BF16),
        ),
        in_specs=[
            pl.BlockSpec((1, some, LOW), lambda i: (0, i, 0)),
            pl.BlockSpec((LOW, 512), lambda i: (0, 0)),
            pl.BlockSpec((96, 512), lambda i: (0, 0)),
            pl.BlockSpec((1, 256, 512), lambda i: (0, 0, 0)),
        ],
        out_specs=(
            pl.BlockSpec((96, 512), lambda i: (0, 0)),
            pl.BlockSpec((1, 256, 512), lambda i: (0, 0, 0)),
            pl.BlockSpec((1, some, 512), lambda i: (0, i, 0)),
        ),
        compiler_params=pltpu.CompilerParams(vmem_limit_bytes=65400 * 1024),
    )(inverse_low, reduced_low, solved_root, solved_mid)


def solution(mesh):
    placed = (
        P("front", "subtree"),
        P(("subtree", "front"), None),
        P(None, ("subtree", "front")),
        P(("subtree", "front")),
        P("subtree", "front", None),
        P("subtree", None, "front"),
        P("subtree", "front", None),
        P("subtree", None, "front"),
        P("subtree", "front"),
        P("subtree", None),
        P(("subtree", "front"), None, None),
        P(("subtree", "front"), None, None),
        P(("subtree", "front"), None, None),
        P(("subtree", "front"), None, None),
        P(("subtree", "front"), None, None),
        P(("subtree", "front"), None),
        P(("subtree", "front"), None),
        P(("subtree", "front"), None),
    )
    return jax.shard_map(
        on_device,
        mesh=mesh,
        in_specs=placed,
        out_specs=(
            P(("subtree", "front"), None),
            P("subtree", "front", None),
            P(("subtree", "front"), None, None),
        ),
        check_vma=False,
    )
```
